32 devices in a mesh: tok: 8 (over z, core), req: 4 (over y, x).
Axes of the slice: x: 2, y: 2, z: 4, core: 2. Of those that a mesh axis runs over, the one named last changes fastest.
Arguments:
- query_rows: bfloat16 [4, 2048, 7168], P('req', 'tok'), may hold values from -16 to 16
- key_rows: bfloat16 [4, 2048, 7168], P('req', 'tok'), may hold values from -16 to 16
- value_rows: bfloat16 [4, 2048, 7168], P('req', 'tok'), may hold values from -6 to 6
- lengths: int32 [4, 6], P('req'), may hold values from 1 to 1024, 2048 in all within a row
- cache_blocks: bfloat16 [4, 64, 2, 32, 3584], P('req', 'tok'), may hold values from -6 to 6
- destinations: int32 [4, 64, 1], P('req', 'tok'), may hold values from 0 to 3; in each aligned block of 8 rows (0 to 7, 8 to 15, ..., all dimensions but the last counted through in order) at most 2 rows name the same one
Outputs:
- attended: bfloat16 [4, 2048, 7168], P('req', 'tok')
- moved_cache: bfloat16 [4, 4, 2, 2, 8, 32, 3584], P('req', None, None, None, None, 'tok')
The draws below stay inside these ranges and needn't reach their ends.
Inputs may be any that keep to these rules, and one draw needn't show every extreme that they name: The 6 lengths of each span sum to 2048, and the longest of every span is exactly 1024. `destinations`: of the 8 rows of one device (aligned blocks of 8 rows), at most 2 name the same group, and in every draw some device names one group exactly 2 times.
All inputs are finite; a program needn't handle non-finite values.
Results may differ from the reference program's by a relative error of at most 0.0037.
Values may be sent and summed in bfloat16 or wider, within the bound.
No kernel may reach another device: no remote copies, remote signals or barrier semaphores. Data moves between devices by JAX's collectives and lax.ppermute only.
A program may use at most 192 MiB of HBM per device.

```python
import math
import jax
import jax.numpy as jnp
import numpy as np
from jax import lax

H = 32
HD = 224
NSEQ = 6
BPD = 8
CAP = 2
SPAN = 2048
SPANS = 4
LONGEST = 1024
BH = 3584
N_TOK = 8
N_REQ = 4


def drawn_pair(key):
    base = jax.random.fold_in(key, 4711)
    key_query, key_keys = jax.random.split(base, 2)
    shape = (SPANS, SPAN, H, HD)
    query_draw = jnp.clip(jax.random.normal(key_query, shape, jnp.float32), -6.0, 6.0)
    key_draw = jnp.clip(jax.random.normal(key_keys, shape, jnp.float32), -6.0, 6.0)
    query_draw = jnp.clip(query_draw, -16.0, 16.0).reshape(SPANS, SPAN, H * HD)
    key_draw = jnp.clip(key_draw, -16.0, 16.0).reshape(SPANS, SPAN, H * HD)
    return (query_draw, key_draw)


def draw_query_rows(key, part):
    return drawn_pair(key)[0].astype(jnp.bfloat16)


def draw_key_rows(key, part):
    return drawn_pair(key)[1].astype(jnp.bfloat16)


def block_levels(key, extent, pieces, least, largest):
    loudness = 1.0
    for position, blocks in pieces:
        heights = jax.random.uniform(jax.random.fold_in(jax.random.fold_in(key, 6), position), (blocks,), jnp.float32, least / len(pieces), largest / len(pieces))
        loudness = loudness * jnp.repeat(jnp.exp(heights), extent[position] // blocks).reshape((-1,) + (1,) * (len(extent) - 1 - position))
    return loudness


def profile(amount, total, limit, skew):
    loads = [(1 << 20) // math.isqrt(standing ** skew) + 1 for standing in range(2, amount + 1)]
    spare, counts = total - limit - (amount - 1), [1] * (amount - 1)
    while spare > 0:
        candidates = [i for i in range(amount - 1) if counts[i] < limit]
        whole, left = sum([loads[i] for i in candidates]), spare
        for i in candidates:
            extra = min(limit - counts[i], max(1, left * loads[i] // whole), spare)
            counts[i] = counts[i] + extra
            spare = spare - extra
    return np.array([limit] + counts)


def ragged(stream_key, number_of, total, bound, slope):
    if number_of == 2:
        one = jax.random.randint(stream_key, (), max(1, total - bound), min(bound, total - 1) + 1)
        return jnp.stack([one, total - one])
    sizes = jnp.asarray(profile(number_of, total, bound, slope), jnp.int32)
    twos = (number_of - 1) // 2
    donor, receiver = sizes[1:1 + 2 * twos:2], sizes[2:2 + 2 * twos:2]
    slack = jnp.minimum(donor - 1, bound - receiver)
    passed = jax.random.randint(jax.random.fold_in(stream_key, 1), (twos,), 0, 1 << 20) % (slack + 1)
    sizes = sizes.at[1:1 + 2 * twos:2].set(donor - passed).at[2:2 + 2 * twos:2].set(receiver + passed)
    return sizes[jax.random.permutation(jax.random.fold_in(stream_key, 2), number_of)]


def routed_block(rng, own, number, rows, amount, top, most, lean):
    order = jax.random.permutation(rng, amount)
    heavy_load, usual = portions_of(amount, rows * top, most, lean, True), portions_of(amount, rows * top, most, lean, False)
    places = jnp.arange(amount)

    def named(sizes, rotation):
        used = int((sizes > 0).sum())
        fixed = max(1, used // 4)
        shifted = fixed + (places - fixed + rotation * (used - fixed)) % max(1, amount - fixed)
        return jnp.zeros((amount,), jnp.int32).at[order[jnp.where(places < fixed, places, shifted)]].set(jnp.asarray(sizes, jnp.int32))

    sizes = jnp.where(number % 4 == 0, named(heavy_load, number // 4), named(usual, number - number // 4 - 1))
    mixed = jax.random.permutation(jax.random.fold_in(own, 3), amount)
    giver, taker = mixed[0:amount // 2 * 2:2], mixed[1:amount // 2 * 2:2]
    room = jnp.minimum(sizes[giver] - 1, most - sizes[taker]) // 2
    room = jnp.where((giver == order[0]) | (taker == order[0]) | (sizes[taker] == 0), 0, jnp.maximum(room, 0))
    shifted = jax.random.randint(jax.random.fold_in(own, 4), (amount // 2,), 0, 1 << 20) % (room + 1)
    sizes = sizes.at[giver].add(-shifted).at[taker].add(shifted)
    items = jnp.searchsorted(jnp.cumsum(sizes), jnp.arange(rows * top), side="right").astype(jnp.int32)
    table = items.reshape(top, rows).T
    table = table[jax.random.permutation(jax.random.fold_in(own, 1), rows)]
    rotation = jax.random.randint(jax.random.fold_in(own, 2), (rows, 1), 0, top)
    return jnp.take_along_axis(table, (jnp.arange(top)[None, :] + rotation) % top, axis=1)


def portions_of(count, total, most, lean, full):
    loads = [(1 << 20) // math.isqrt(grade ** lean) + 1 for grade in range(1, count + 1)]
    largest = most if full else min(most, max(-(-total // count), total * loads[0] // sum(loads)))
    least = 1 if total - largest >= count - 1 else 0
    counts, surplus = [largest] + [least] * (count - 1), total - largest - least * (count - 1)
    while surplus > 0:
        candidates = [i for i in range(1, count) if counts[i] < largest] or [i for i in range(1, count) if counts[i] < most]
        pool, remaining = sum([loads[i] for i in candidates]), surplus
        for i in candidates:
            more = min(most - counts[i], max(1, remaining * loads[i] // pool), surplus)
            counts[i] = counts[i] + more
            surplus = surplus - more
    return np.array(counts)


def centred(rng, dims, width, bound, cuts=(), held_as=jnp.bfloat16):
    array = jax.random.normal(rng, dims, jnp.float32) * width
    if len(cuts) > 0:
        array = block_levels(rng, dims, cuts, -0.22, 0.18) * array
    return jnp.clip(array, min=-bound, max=bound).astype(held_as)


def setup_inputs(seed: int = 0) -> dict:
    seeds = jax.random.split(jax.random.key(seed), 7)
    query_rows = draw_query_rows(jax.random.fold_in(seeds[6], 71), 0)
    key_rows = draw_key_rows(jax.random.fold_in(seeds[6], 71), 0)
    value_rows = centred(seeds[2], (SPANS, SPAN, H * HD), 1.0, 6.0, ((0, 4), (1, 8)))
    lengths = jax.vmap(lambda own: ragged(own, NSEQ, SPAN, LONGEST, 2))(jax.random.split(seeds[3], SPANS)).reshape((SPANS, NSEQ)).astype(jnp.int32)
    cache_blocks = centred(seeds[4], (N_REQ, N_TOK * BPD, 2, H, BH), 1.0, 6.0, ((0, 4), (1, 8)))
    destinations_keys = jax.random.split(jax.random.fold_in(seeds[5], 1), N_REQ * (N_TOK * BPD) // BPD)
    destinations_turns = jax.random.permutation(jax.random.fold_in(seeds[5], 3), N_REQ * (N_TOK * BPD) // BPD)
    destinations = jax.vmap(lambda own, number: routed_block(jax.random.fold_in(seeds[5], 2), own, number, BPD, N_REQ, 1, CAP, 2))(destinations_keys, destinations_turns).reshape((N_REQ, N_TOK * BPD, 1))
    return {"query_rows": query_rows, "key_rows": key_rows, "value_rows": value_rows, "lengths": lengths, "cache_blocks": cache_blocks, "destinations": destinations}


def segment_ids(lengths):
    ends = jnp.cumsum(lengths, axis=-1)
    positions = jnp.arange(SPAN, dtype=jnp.int32)
    return jnp.sum((positions[None, :, None] >= ends[:, None, :]).astype(jnp.int32), axis=-1)


def head_attend(query_head, key_head, value_head, segments):
    positions = jnp.arange(query_head.shape[0], dtype=jnp.int32)
    scores = jnp.dot(query_head, key_head.T, preferred_element_type=jnp.float32) * (query_head.shape[1] ** -0.5)
    visible = (segments[:, None] == segments[None, :]) & (positions[:, None] >= positions[None, :])
    scores = jnp.where(visible, scores, -1e30)
    row_max = jnp.max(scores, axis=1, keepdims=True)
    weights = jnp.where(visible, jnp.exp(scores - row_max), 0.0)
    row_total = jnp.sum(weights, axis=1, keepdims=True)
    summed = jnp.dot(weights.astype(jnp.bfloat16), value_head, preferred_element_type=jnp.float32)
    return (summed / row_total).astype(jnp.bfloat16)


def relocate(cache_blocks, destinations):
    targets = destinations[..., 0].reshape(N_REQ, N_TOK, BPD)
    positions = jnp.arange(BPD, dtype=jnp.int32)
    earlier = (targets[..., :, None] == targets[..., None, :]) & (positions[None, :] < positions[:, None])
    slot_rank = jnp.sum(earlier.astype(jnp.int32), axis=-1)
    target_swap = jnp.transpose(targets, (1, 0, 2))
    rank_swap = jnp.transpose(slot_rank, (1, 0, 2))
    groups = jnp.arange(N_REQ, dtype=jnp.int32)
    slots = jnp.arange(CAP, dtype=jnp.int32)
    match = (target_swap[None, :, :, None, :] == groups[:, None, None, None, None]) & (rank_swap[None, :, :, None, :] == slots[None, None, None, :, None])
    which = jnp.sum(jnp.where(match, positions, 0), axis=-1).astype(jnp.int32)
    valid = jnp.any(match, axis=-1)
    row_index = jnp.arange(N_TOK, dtype=jnp.int32)[None, :, None, None] * BPD + which
    source_index = jnp.arange(N_REQ, dtype=jnp.int32)[None, None, :, None] + 0 * row_index
    picked = cache_blocks[source_index, row_index]
    placed = jnp.where(valid[..., None, None, None], picked, jnp.zeros((), cache_blocks.dtype))
    return jnp.transpose(placed, (0, 2, 3, 4, 1, 5, 6))


def reference(query_rows, key_rows, value_rows, lengths, cache_blocks, destinations):
    segments = segment_ids(lengths)

    def to_heads(rows_in):
        return jnp.transpose(rows_in.reshape(SPANS, SPAN, H, HD), (0, 2, 1, 3))

    def one_span(item):
        query_span, key_span, value_span, span_segments = item

        def one_head(parts):
            return head_attend(parts[0], parts[1], parts[2], span_segments)

        return lax.map(one_head, (query_span, key_span, value_span))

    heads = lax.map(one_span, (to_heads(query_rows), to_heads(key_rows), to_heads(value_rows), segments))
    attended = jnp.transpose(heads, (0, 2, 1, 3)).reshape(SPANS, SPAN, H * HD)
    moved_cache = relocate(cache_blocks, destinations)
    return (attended, moved_cache)
```

```python
import functools
import math

import jax
import jax.numpy as jnp
from jax import lax
from jax.experimental import pallas as pl
from jax.experimental.pallas import tpu as pltpu
from jax.sharding import PartitionSpec as P

HD = 224
CAP = 2
GROUP = 4
WIDTH = GROUP * HD
NEG = -1e30
FLOOR = -1e29
EXP2_SCALE = HD**-0.5 * math.log2(math.e)
STAT_ROWS = 16
TILE = 32
WINDOWS = tuple((h * HD // 128 * 128, -(-(h + 1) * HD // 128) * 128) for h in range(GROUP))


def starts_of(ends_ref, count, position):
    start = jnp.zeros_like(position)
    for i in range(count):
        end = ends_ref[i]
        start = jnp.where(position >= end, end, start)
    return start


def lanes_of(head, rows):
    low, high = WINDOWS[head]
    lane = lax.broadcasted_iota(jnp.int32, (rows, high - low), 1) + low
    return (lane >= head * HD) & (lane < (head + 1) * HD)


def attend_block(ends_ref, count, query_ref, row, base, key_refs, m_ref, l_ref, acc_ref, work):
    scores_ref, weights_ref, hidden_ref, decay_ref = work
    rows = m_ref.shape[1]
    lowest = starts_of(ends_ref, count, base)
    m_ref[...] = jnp.full(m_ref.shape, FLOOR, jnp.float32)
    l_ref[...] = jnp.zeros(l_ref.shape, jnp.float32)
    acc_ref[...] = jnp.zeros(acc_ref.shape, jnp.float32)
    for key_ref, bases, usable in key_refs:
        depth = key_ref.shape[0] // 2
        begin = jnp.minimum(bases[0], bases[1])
        needed = usable & (lowest < begin + depth) & (base + rows > begin)

        @pl.when(needed)
        def _(key_ref=key_ref, bases=bases, depth=depth):
            column = lax.broadcasted_iota(jnp.int32, (1, depth), 1)
            key_position = jnp.where(column < depth // 2, bases[0] + column, bases[1] + column - depth // 2)
            for tile in range(0, rows, TILE):
                position = base + tile + lax.broadcasted_iota(jnp.int32, (TILE, 1), 0)
                first = starts_of(ends_ref, count, position)
                visible = (key_position <= position) & (key_position >= first)
                hidden_ref[tile : tile + TILE] = jnp.where(visible, 0.0, NEG)
            for head in range(GROUP):
                low, high = WINDOWS[head]
                query = query_ref[pl.ds(row, rows), low:high]
                query = jnp.where(lanes_of(head, rows), query, jnp.zeros((), query.dtype))
                scores_ref[head] = lax.dot_general(
                    query, key_ref[:depth, low:high], (((1,), (1,)), ((), ())), preferred_element_type=jnp.float32
                )
            for head in range(GROUP):
                low, high = WINDOWS[head]
                for tile in range(0, rows, TILE):
                    part = slice(tile, tile + TILE)
                    scores = scores_ref[head, part] + hidden_ref[part]
                    old = m_ref[head, part]
                    new = jnp.maximum(old, jnp.max(scores, axis=1, keepdims=True))
                    weights = jnp.exp2((scores - new[:, :1]) * EXP2_SCALE)
                    decay = jnp.exp2((old - new) * EXP2_SCALE)
                    m_ref[head, part] = new
                    decay_ref[head, part] = decay
                    l_ref[head, part] = l_ref[head, part] * decay + jnp.sum(weights, axis=1, keepdims=True)
                    weights_ref[head, part] = weights.astype(jnp.bfloat16)
                summed = jnp.dot(weights_ref[head], key_ref[depth:, low:high], preferred_element_type=jnp.float32)
                for lane in range(0, high - low, 128):
                    lanes = slice(lane, lane + 128)
                    acc_ref[head, :, lanes] = acc_ref[head, :, lanes] * decay_ref[head] + summed[:, lanes]


def place(out_ref, row, rows, head, value, scratch_ref):
    low, high = WINDOWS[head]
    lane = lax.broadcasted_iota(jnp.int32, (rows, high - low), 1) + low
    if head > 0:
        value = jnp.where(lane >= head * HD, value, scratch_ref[:, low:high])
    scratch_ref[:, low:high] = value
    if head == GROUP - 1:
        out_ref[pl.ds(row, rows), :] = scratch_ref[...].astype(jnp.bfloat16)


def remote_kernel(
    count, block, meta_ref, ends_ref, near_ref, far_ref, own_ref, prev_ref, near_out, far_out, m_ref, l_ref, acc_ref, row_ref, *work
):
    own = (own_ref, (meta_ref[0], meta_ref[1]), meta_ref[6] > 0)
    prev = (prev_ref, (meta_ref[2], meta_ref[3]), meta_ref[7] > 0)
    depth = own_ref.shape[0] // 2
    for query_ref, out_ref, hops, enabled in ((near_ref, near_out, 1, meta_ref[4]), (far_ref, far_out, 2, meta_ref[5])):

        @pl.when(enabled > 0)
        def _(query_ref=query_ref, out_ref=out_ref, hops=hops):
            @pl.loop(0, 2)
            def _(i):
                row = pl.multiple_of(i * block, block)
                base = jnp.where(i == 0, meta_ref[0], meta_ref[1]) + hops * depth
                attend_block(ends_ref, count, query_ref, row, base, (own, prev), m_ref, l_ref, acc_ref, work)
                lane = lax.broadcasted_iota(jnp.int32, (block, 128), 1)
                stats = jnp.zeros((block, 128), jnp.float32)
                for head in range(GROUP):
                    low, high = WINDOWS[head]
                    total = l_ref[head][:, :1]
                    empty = total == 0.0
                    safe = jnp.where(empty, 1.0, total)
                    place(out_ref, row, block, head, acc_ref[head, :, : high - low] / safe, row_ref)
                    level = jnp.where(empty, NEG, m_ref[head][:, :1] * EXP2_SCALE + jnp.log2(safe))
                    for part in range(3):
                        piece = level.astype(jnp.bfloat16).astype(jnp.float32)
                        stats = jnp.where(lane == part * GROUP + head, piece, stats)
                        level = level - piece
                flat = jnp.transpose(stats)[:STAT_ROWS].astype(jnp.bfloat16)
                out_ref[2 * block :, pl.ds(row, block)] = flat


def home_kernel(
    count, block, meta_ref, ends_ref, query_ref, own_ref, prev_ref, near_ref, far_ref, mine_out, other_out, m_ref, l_ref, acc_ref, row_ref, *work
):
    own = (own_ref, (meta_ref[0], meta_ref[1]), meta_ref[6] > 0)
    prev = (prev_ref, (meta_ref[2], meta_ref[3]), meta_ref[7] > 0)
    for i, out_ref in enumerate((mine_out, other_out)):
        row = i * block
        attend_block(ends_ref, count, query_ref, row, meta_ref[i], (own, prev), m_ref, l_ref, acc_ref, work)
        parts = []
        for part_ref, enabled in ((near_ref, meta_ref[8]), (far_ref, meta_ref[9])):
            stats = jnp.transpose(part_ref[2 * block :, row : row + block].astype(jnp.float32))
            parts.append((part_ref, stats, enabled > 0))
        for head in range(GROUP):
            low, high = WINDOWS[head]
            level = m_ref[head][:, :1] * EXP2_SCALE
            others = []
            for part_ref, stats, enabled in parts:
                theirs = stats[:, head : head + 1] + stats[:, GROUP + head : GROUP + head + 1]
                theirs = theirs + stats[:, 2 * GROUP + head : 2 * GROUP + head + 1]
                others.append((part_ref, jnp.where(enabled, theirs, NEG)))
            top = jnp.maximum(jnp.maximum(level, others[0][1]), others[1][1])
            weight = jnp.exp2(level - top)
            total = l_ref[head][:, :1] * weight
            value = acc_ref[head, :, : high - low] * weight
            for part_ref, theirs in others:
                weight = jnp.exp2(theirs - top)
                total = total + weight
                value = value + part_ref[row : row + block, low:high].astype(jnp.float32) * weight
            place(out_ref, 0, block, head, value / total, row_ref)


def scratch(block):
    widest = max(high - low for low, high in WINDOWS)
    return [
        pltpu.VMEM((GROUP, block, 128), jnp.float32),
        pltpu.VMEM((GROUP, block, 128), jnp.float32),
        pltpu.VMEM((GROUP, block, widest), jnp.float32),
        pltpu.VMEM((block, WIDTH), jnp.float32),
        pltpu.VMEM((GROUP, block, 2 * block), jnp.float32),
        pltpu.VMEM((GROUP, block, 2 * block), jnp.bfloat16),
        pltpu.VMEM((block, 2 * block), jnp.float32),
        pltpu.VMEM((GROUP, block, 128), jnp.float32),
    ]


def call(kernel, count, block, outs, arrays, flops):
    smem = pl.BlockSpec(memory_space=pltpu.SMEM)
    vmem = pl.BlockSpec(memory_space=pltpu.VMEM)
    return pl.pallas_call(
        functools.partial(kernel, count, block),
        out_shape=[jax.ShapeDtypeStruct(shape, jnp.bfloat16) for shape in outs],
        in_specs=[smem, smem] + [vmem] * (len(arrays) - 2),
        out_specs=[vmem] * len(outs),
        scratch_shapes=scratch(block),
        compiler_params=pltpu.CompilerParams(vmem_limit_bytes=40 * 1024 * 1024),
        cost_estimate=pl.CostEstimate(flops=flops, bytes_accessed=8 * 1024 * 1024, transcendentals=flops // 1000),
    )(*arrays)


def after(arrays, earlier):
    return lax.optimization_barrier((tuple(arrays), tuple(earlier)))[0]


def attend_chips(query_rows, key_rows, value_rows, lengths, cache_blocks, targets):
    index = lax.axis_index("tok")
    core = index % 2
    chip = index // 2
    block, feature = query_rows.shape
    half = feature // 2
    chunks = half // WIDTH
    count = lengths.shape[0]
    ends = jnp.cumsum(lengths).astype(jnp.int32)
    swap = [(i, i ^ 1) for i in range(8)]

    def own_half(rows):
        return jnp.where(core == 0, rows[:, :half], rows[:, half:])

    def other_half(rows):
        return jnp.where(core == 0, rows[:, half:], rows[:, :half])

    def cut(rows, j):
        return rows[:, j * WIDTH : (j + 1) * WIDTH]

    def shared(rows):
        mine = own_half(rows)
        other = lax.ppermute(other_half(rows), "tok", swap)
        return mine, other

    query, key, value = shared(query_rows), shared(key_rows), shared(value_rows)
    first = chip * 2 * block
    bases = [first + core * block, first + (1 - core) * block]
    meta = jnp.stack(
        bases
        + [b - 2 * block for b in bases]
        + [(chip == 1) | (chip == 2), chip == 1, chip >= 0, chip == 1, chip >= 2, chip == 3]
    ).astype(jnp.int32)
    near_left = [(i, i - 2) for i in range(4, 8)]
    far_left = [(i, i - 4) for i in range(6, 8)]
    near_right = [(j, i) for i, j in near_left]
    far_right = [(j, i) for i, j in far_left]
    first_right = [(0, 2), (1, 3)]
    rows_out = 2 * block + STAT_ROWS
    flops = 4 * 512 * 512 * 224 * 4 * 2
    queries, keys, near, far, keys_before, near_back, far_back, mine, other = ([] for _ in range(9))
    for j in range(chunks):
        queries.append(jnp.concatenate([cut(query[0], j), cut(query[1], j)], axis=0))
        keys.append(jnp.concatenate([cut(key[0], j), cut(key[1], j), cut(value[0], j), cut(value[1], j)], axis=0))

    def send(j, previous):
        out_queries, out_keys = (queries[j], keys[j]) if previous is None else after((queries[j], keys[j]), previous)
        near.append(lax.ppermute(out_queries, "tok", near_left))
        far.append(lax.ppermute(out_queries, "tok", far_left))
        keys_before.append(lax.ppermute(out_keys, "tok", first_right))

    def home(j):
        out_mine, out_other = call(
            home_kernel, count, block, [(block, WIDTH)] * 2,
            [meta, ends, queries[j], keys[j], keys_before[j], near_back[j], far_back[j]], flops,
        )
        mine.append(out_mine)
        other.append(out_other)

    send(0, None)
    moves = CacheMoves(cache_blocks, targets, queries[0])
    send(1, (near[0], far[0], keys_before[0], moves.outgoing))
    moves.early()
    for j in range(chunks):
        parts = call(
            remote_kernel, count, block, [(rows_out, WIDTH)] * 2,
            [meta, ends, near[j], far[j], keys[j], keys_before[j]], flops,
        )
        back = (near_back[-1], far_back[-1]) if j > 0 else (moves.one, moves.two)
        near_part, far_part = after(parts, back)
        near_back.append(lax.ppermute(near_part, "tok", near_right))
        far_back.append(lax.ppermute(far_part, "tok", far_right))
        if j > 1:
            home(j - 2)
        if j + 1 < chunks:
            earlier = (near[j + 1], far[j + 1], keys_before[j + 1]) + tuple(parts) + back + tuple(mine[-1:])
            if j + 2 < chunks:
                send(j + 2, earlier)
            else:
                moves.late(earlier)
    for j in range(chunks - 2, chunks):
        home(j)
    mine, other = jnp.concatenate(mine, axis=1), jnp.concatenate(other, axis=1)
    other = lax.ppermute(other, "tok", swap)
    low, high = jnp.where(core == 0, mine, other), jnp.where(core == 0, other, mine)
    return jnp.concatenate([low, high], axis=1), moves.result()


def assemble_kernel(places_ref, here_ref, one_ref, two_ref, three_ref, early_ref, partner_ref, out_ref):
    core = places_ref[0]
    for i, piece_ref in enumerate((here_ref, one_ref, two_ref, three_ref)):
        chip, early = places_ref[1 + i], places_ref[5 + i]
        out_ref[:, pl.ds(2 * chip + 1 - core, 1)] = partner_ref[:, i : i + 1]

        @pl.when(early > 0)
        def _(i=i, chip=chip):
            out_ref[:, pl.ds(2 * chip + core, 1)] = early_ref[:, (0, 0, 1, 0)[i], pl.ds(core, 1)]

        @pl.when(early == 0)
        def _(piece_ref=piece_ref, chip=chip):
            out_ref[:, pl.ds(2 * chip + core, 1)] = piece_ref[:, pl.ds(core, 1)]


class CacheMoves:
    def __init__(self, cache_blocks, targets, earlier):
        self.groups = lax.axis_size("req")
        index = lax.axis_index("tok")
        self.chip, self.core = index // 2, index % 2
        (cache_blocks, targets) = after((cache_blocks, targets), (earlier,))
        placing = slots_of(targets, self.groups, cache_blocks.dtype)
        block_count, kinds, heads, entries = cache_blocks.shape
        local = cache_blocks.reshape(block_count, kinds, 4, 2, heads // 8, entries)
        outgoing = jnp.einsum("bdc,bjtkhy->dtcjkhy", placing, local, preferred_element_type=jnp.float32)
        self.outgoing = outgoing.astype(jnp.bfloat16)
        self.flat = (self.groups * CAP * kinds, 2, heads // 8, entries)

    def early(self):
        def piece(chip):
            return lax.dynamic_index_in_dim(self.outgoing, jnp.minimum(chip, 3), axis=1, keepdims=False)

        self.one = lax.ppermute(piece(self.chip + 1), "tok", [(2, 4), (3, 5), (4, 6), (5, 7)])
        self.two = lax.ppermute(piece(self.chip + 2), "tok", [(2, 6), (3, 7)])
        self.grouped = lax.all_to_all(self.outgoing, "req", split_axis=0, concat_axis=0, tiled=True)
        both = jnp.stack([self.one, self.two], axis=1)
        self.arrived = lax.all_to_all(both, "req", split_axis=0, concat_axis=0, tiled=True)

    def late(self, earlier):
        (grouped,) = after((self.grouped,), earlier)

        def piece(distance):
            return lax.dynamic_index_in_dim(grouped, self.chip ^ distance, axis=1, keepdims=False)

        def exchange(distance, skipped):
            pairs = [(i, i ^ (2 * distance)) for i in range(8) if i // 2 not in skipped]
            return lax.ppermute(piece(distance), "tok", pairs)

        self.pieces = [piece(0), exchange(1, (2,)), exchange(2, (1,)), exchange(3, (1,))]

    def result(self):
        shape = self.flat
        chip, core = self.chip, self.core
        pieces = [p.reshape(shape) for p in self.pieces]
        arrived = self.arrived.reshape((self.groups, 2, -1) + shape[1:])
        arrived = jnp.transpose(arrived, (0, 2, 1, 3, 4, 5)).reshape((shape[0], 2) + shape[1:])
        early = [chip < 0, chip == 3, chip == 3, chip == 2]
        sent = []
        for i, piece in enumerate(pieces):
            if i > 0:
                piece = jnp.where(early[i], arrived[:, (0, 0, 1, 0)[i]], piece)
            sent.append(jnp.where(core == 0, piece[:, 1], piece[:, 0]))
        partner = lax.ppermute(jnp.stack(sent, axis=1), "tok", [(i, i ^ 1) for i in range(8)])
        places = jnp.stack([core] + [chip ^ d for d in range(4)] + early).astype(jnp.int32)
        step = 2

        def blocks(array):
            return pl.BlockSpec((step,) + array.shape[1:], lambda i: (i,) + (0,) * (array.ndim - 1))

        arrays = (*pieces, arrived, partner)
        out = jax.ShapeDtypeStruct((shape[0], 8) + shape[2:], jnp.bfloat16)
        out = pl.pallas_call(
            assemble_kernel,
            out_shape=out,
            grid=(shape[0] // step,),
            in_specs=[pl.BlockSpec(memory_space=pltpu.SMEM)] + [blocks(array) for array in arrays],
            out_specs=blocks(out),
            compiler_params=pltpu.CompilerParams(vmem_limit_bytes=40 * 1024 * 1024),
        )(places, *arrays)
        return out.reshape((self.groups, CAP, -1) + out.shape[1:])


def attend_heads_all(query_rows, key_rows, value_rows, lengths):
    tok_count = lax.axis_size("tok")
    rows, feature = query_rows.shape
    group = feature // tok_count
    length = rows * tok_count

    def regroup(array):
        return lax.all_to_all(array, "tok", split_axis=1, concat_axis=0, tiled=True)

    query, key, value = regroup(query_rows), regroup(key_rows), regroup(value_rows)
    ends = jnp.cumsum(lengths)
    position = jnp.arange(length, dtype=jnp.int32)
    segments = jnp.sum((position[:, None] >= ends[None, :]).astype(jnp.int32), axis=1)
    block = min(512, length)
    blocks = []
    for low in range(0, length, block):
        high = low + block
        visible = (segments[low:high, None] == segments[None, :high]) & (position[low:high, None] >= position[None, :high])
        heads = []
        for head in range(group // HD):
            lanes = slice(head * HD, (head + 1) * HD)
            scores = lax.dot_general(
                query[low:high, lanes], key[:high, lanes], (((1,), (1,)), ((), ())), preferred_element_type=jnp.float32
            )
            scores = jnp.where(visible, scores * HD**-0.5, NEG)
            weights = jnp.where(visible, jnp.exp(scores - jnp.max(scores, axis=1, keepdims=True)), 0.0)
            total = jnp.sum(weights, axis=1, keepdims=True)
            summed = jnp.dot(weights.astype(jnp.bfloat16), value[:high, lanes], preferred_element_type=jnp.float32)
            heads.append((summed / total).astype(jnp.bfloat16))
        blocks.append(jnp.concatenate(heads, axis=1))
    return lax.all_to_all(jnp.concatenate(blocks, axis=0), "tok", split_axis=0, concat_axis=1, tiled=True)


def slots_of(targets, groups, dtype):
    positions = jnp.arange(targets.shape[0], dtype=jnp.int32)
    earlier = (targets[:, None] == targets[None, :]) & (positions[None, :] < positions[:, None])
    slot_rank = jnp.sum(earlier.astype(jnp.int32), axis=1)
    return (
        (targets[:, None, None] == jnp.arange(groups, dtype=jnp.int32)[None, :, None])
        & (slot_rank[:, None, None] == jnp.arange(CAP, dtype=jnp.int32)[None, None, :])
    ).astype(dtype)


def relocate(cache_blocks, targets):
    groups = lax.axis_size("req")
    tok_count = lax.axis_size("tok")
    block_count, kinds, heads, entries = cache_blocks.shape
    placing = slots_of(targets, groups, cache_blocks.dtype)
    here = heads // tok_count
    local = cache_blocks.reshape(block_count, kinds, tok_count, here, entries)
    outgoing = jnp.einsum("bdc,bjthy->dtcjhy", placing, local, preferred_element_type=jnp.float32).astype(jnp.bfloat16)
    outgoing = outgoing.reshape(groups * tok_count, CAP, kinds, here, entries)
    arrived = lax.all_to_all(outgoing, ("req", "tok"), split_axis=0, concat_axis=0, tiled=True)
    arrived = arrived.reshape(groups, tok_count, CAP, kinds, here, entries)
    return jnp.transpose(arrived, (0, 2, 3, 1, 4, 5))


def on_device(query_rows, key_rows, value_rows, lengths, cache_blocks, destinations):
    targets = destinations[0, :, 0]
    if lax.axis_size("tok") == 8:
        attended, moved_cache = attend_chips(
            query_rows[0], key_rows[0], value_rows[0], lengths[0], cache_blocks[0], targets
        )
    else:
        attended = attend_heads_all(query_rows[0], key_rows[0], value_rows[0], lengths[0])
        moved_cache = relocate(cache_blocks[0], targets)
    return (attended[None], moved_cache[None])


def solution(mesh):
    return jax.shard_map(
        on_device,
        mesh=mesh,
        in_specs=(
            P("req", "tok", None),
            P("req", "tok", None),
            P("req", "tok", None),
            P("req", None),
            P("req", "tok", None, None, None),
            P("req", "tok", None),
        ),
        out_specs=(P("req", "tok", None), P("req", None, None, None, None, "tok", None)),
        check_vma=False,
    )
```

```python
import functools
import math

import jax
import jax.numpy as jnp
from jax import lax
from jax.experimental import pallas as pl
from jax.experimental.pallas import tpu as pltpu
from jax.sharding import PartitionSpec as P

HD = 224
CAP = 2
GROUP = 4
WIDTH = GROUP * HD
NEG = -1e30
FLOOR = -1e29
EXP2_SCALE = HD**-0.5 * math.log2(math.e)
STAT_ROWS = 16
TILE = 32
WINDOWS = tuple((h * HD // 128 * 128, -(-(h + 1) * HD // 128) * 128) for h in range(GROUP))


def starts_of(ends_ref, count, position):
    start = jnp.zeros_like(position)
    for i in range(count):
        end = ends_ref[i]
        start = jnp.where(position >= end, end, start)
    return start


def lanes_of(head, rows):
    low, high = WINDOWS[head]
    lane = lax.broadcasted_iota(jnp.int32, (rows, high - low), 1) + low
    return (lane >= head * HD) & (lane < (head + 1) * HD)


def attend_block(ends_ref, count, query_ref, row, base, key_refs, m_ref, l_ref, acc_ref, work):
    scores_ref, weights_ref, hidden_ref, decay_ref = work
    rows = m_ref.shape[1]
    lowest = starts_of(ends_ref, count, base)
    m_ref[...] = jnp.full(m_ref.shape, FLOOR, jnp.float32)
    l_ref[...] = jnp.zeros(l_ref.shape, jnp.float32)
    acc_ref[...] = jnp.zeros(acc_ref.shape, jnp.float32)
    for key_ref, bases, usable in key_refs:
        depth = key_ref.shape[0] // 2
        begin = jnp.minimum(bases[0], bases[1])
        needed = usable & (lowest < begin + depth) & (base + rows > begin)

        @pl.when(needed)
        def _(key_ref=key_ref, bases=bases, depth=depth):
            column = lax.broadcasted_iota(jnp.int32, (1, depth), 1)
            key_position = jnp.where(column < depth // 2, bases[0] + column, bases[1] + column - depth // 2)
            for tile in range(0, rows, TILE):
                position = base + tile + lax.broadcasted_iota(jnp.int32, (TILE, 1), 0)
                first = starts_of(ends_ref, count, position)
                visible = (key_position <= position) & (key_position >= first)
                hidden_ref[tile : tile + TILE] = jnp.where(visible, 0.0, NEG)
            for head in range(GROUP):
                low, high = WINDOWS[head]
                query = query_ref[pl.ds(row, rows), low:high]
                query = jnp.where(lanes_of(head, rows), query, jnp.zeros((), query.dtype))
                scores_ref[head] = lax.dot_general(
                    query, key_ref[:depth, low:high], (((1,), (1,)), ((), ())), preferred_element_type=jnp.float32
                )
            for head in range(GROUP):
                low, high = WINDOWS[head]
                for tile in range(0, rows, TILE):
                    part = slice(tile, tile + TILE)
                    scores = scores_ref[head, part] + hidden_ref[part]
                    old = m_ref[head, part]
                    new = jnp.maximum(old, jnp.max(scores, axis=1, keepdims=True))
                    weights = jnp.exp2((scores - new[:, :1]) * EXP2_SCALE)
                    decay = jnp.exp2((old - new) * EXP2_SCALE)
                    m_ref[head, part] = new
                    decay_ref[head, part] = decay
                    l_ref[head, part] = l_ref[head, part] * decay + jnp.sum(weights, axis=1, keepdims=True)
                    weights_ref[head, part] = weights.astype(jnp.bfloat16)
                summed = jnp.dot(weights_ref[head], key_ref[depth:, low:high], preferred_element_type=jnp.float32)
                for lane in range(0, high - low, 128):
                    lanes = slice(lane, lane + 128)
                    acc_ref[head, :, lanes] = acc_ref[head, :, lanes] * decay_ref[head] + summed[:, lanes]


def place(out_ref, row, rows, head, value, scratch_ref):
    low, high = WINDOWS[head]
    lane = lax.broadcasted_iota(jnp.int32, (rows, high - low), 1) + low
    if head > 0:
        value = jnp.where(lane >= head * HD, value, scratch_ref[:, low:high])
    scratch_ref[:, low:high] = value
    if head == GROUP - 1:
        out_ref[pl.ds(row, rows), :] = scratch_ref[...].astype(jnp.bfloat16)


def remote_kernel(
    count, block, meta_ref, ends_ref, near_ref, far_ref, own_ref, prev_ref, *refs
):
    spare, (one_out, two_out, m_ref, l_ref, acc_ref, row_ref, *work) = refs[:-10], refs[-10:]
    own = (own_ref, (meta_ref[0], meta_ref[1]), meta_ref[6] > 0)
    prev = (prev_ref, (meta_ref[2], meta_ref[3]), meta_ref[7] > 0)
    depth = own_ref.shape[0] // 2
    for query_ref, out_ref, hops, enabled in ((near_ref, two_out, 1, meta_ref[4]), (far_ref, one_out, 2, meta_ref[5])):
        if spare:

            @pl.when(enabled == 0)
            def _(out_ref=out_ref):
                out_ref[...] = spare[0][...]

        @pl.when(enabled > 0)
        def _(query_ref=query_ref, out_ref=out_ref, hops=hops):
            @pl.loop(0, 2)
            def _(i):
                row = pl.multiple_of(i * block, block)
                base = jnp.where(i == 0, meta_ref[0], meta_ref[1]) + hops * depth
                attend_block(ends_ref, count, query_ref, row, base, (own, prev), m_ref, l_ref, acc_ref, work)
                lane = lax.broadcasted_iota(jnp.int32, (block, 128), 1)
                stats = jnp.zeros((block, 128), jnp.float32)
                for head in range(GROUP):
                    low, high = WINDOWS[head]
                    total = l_ref[head][:, :1]
                    empty = total == 0.0
                    safe = jnp.where(empty, 1.0, total)
                    place(out_ref, row, block, head, acc_ref[head, :, : high - low] / safe, row_ref)
                    level = jnp.where(empty, NEG, m_ref[head][:, :1] * EXP2_SCALE + jnp.log2(safe))
                    for part in range(3):
                        piece = level.astype(jnp.bfloat16).astype(jnp.float32)
                        stats = jnp.where(lane == part * GROUP + head, piece, stats)
                        level = level - piece
                flat = jnp.transpose(stats)[:STAT_ROWS].astype(jnp.bfloat16)
                out_ref[2 * block :, pl.ds(row, block)] = flat


def home_kernel(
    count, block, meta_ref, ends_ref, query_ref, own_ref, prev_ref, near_ref, far_ref, mine_out, other_out, m_ref, l_ref, acc_ref, row_ref, *work
):
    own = (own_ref, (meta_ref[0], meta_ref[1]), meta_ref[6] > 0)
    prev = (prev_ref, (meta_ref[2], meta_ref[3]), meta_ref[7] > 0)
    for i, out_ref in enumerate((mine_out, other_out)):
        row = i * block
        attend_block(ends_ref, count, query_ref, row, meta_ref[i], (own, prev), m_ref, l_ref, acc_ref, work)
        parts = []
        for part_ref, enabled in ((near_ref, meta_ref[8]), (far_ref, meta_ref[9])):
            stats = jnp.transpose(part_ref[2 * block :, row : row + block].astype(jnp.float32))
            parts.append((part_ref, stats, enabled > 0))
        for head in range(GROUP):
            low, high = WINDOWS[head]
            level = m_ref[head][:, :1] * EXP2_SCALE
            others = []
            for part_ref, stats, enabled in parts:
                theirs = stats[:, head : head + 1] + stats[:, GROUP + head : GROUP + head + 1]
                theirs = theirs + stats[:, 2 * GROUP + head : 2 * GROUP + head + 1]
                others.append((part_ref, jnp.where(enabled, theirs, NEG)))
            top = jnp.maximum(jnp.maximum(level, others[0][1]), others[1][1])
            weight = jnp.exp2(level - top)
            total = l_ref[head][:, :1] * weight
            value = acc_ref[head, :, : high - low] * weight
            for part_ref, theirs in others:
                weight = jnp.exp2(theirs - top)
                total = total + weight
                value = value + part_ref[row : row + block, low:high].astype(jnp.float32) * weight
            place(out_ref, 0, block, head, value / total, row_ref)


def scratch(block):
    widest = max(high - low for low, high in WINDOWS)
    return [
        pltpu.VMEM((GROUP, block, 128), jnp.float32),
        pltpu.VMEM((GROUP, block, 128), jnp.float32),
        pltpu.VMEM((GROUP, block, widest), jnp.float32),
        pltpu.VMEM((block, WIDTH), jnp.float32),
        pltpu.VMEM((GROUP, block, 2 * block), jnp.float32),
        pltpu.VMEM((GROUP, block, 2 * block), jnp.bfloat16),
        pltpu.VMEM((block, 2 * block), jnp.float32),
        pltpu.VMEM((GROUP, block, 128), jnp.float32),
    ]


def call(kernel, count, block, outs, arrays, flops):
    smem = pl.BlockSpec(memory_space=pltpu.SMEM)
    vmem = pl.BlockSpec(memory_space=pltpu.VMEM)
    return pl.pallas_call(
        functools.partial(kernel, count, block),
        out_shape=[jax.ShapeDtypeStruct(shape, jnp.bfloat16) for shape in outs],
        in_specs=[smem, smem] + [vmem] * (len(arrays) - 2),
        out_specs=[vmem] * len(outs),
        scratch_shapes=scratch(block),
        compiler_params=pltpu.CompilerParams(vmem_limit_bytes=40 * 1024 * 1024),
        cost_estimate=pl.CostEstimate(flops=flops, bytes_accessed=8 * 1024 * 1024, transcendentals=flops // 1000),
    )(*arrays)


def after(arrays, earlier):
    return lax.optimization_barrier((tuple(arrays), tuple(earlier)))[0]


def attend_chips(query_rows, key_rows, value_rows, lengths, cache_blocks, targets):
    index = lax.axis_index("tok")
    core = index % 2
    chip = index // 2
    block, feature = query_rows.shape
    half = feature // 2
    chunks = half // WIDTH
    count = lengths.shape[0]
    ends = jnp.cumsum(lengths).astype(jnp.int32)
    swap = [(i, i ^ 1) for i in range(8)]

    def own_half(rows):
        return jnp.where(core == 0, rows[:, :half], rows[:, half:])

    def other_half(rows):
        return jnp.where(core == 0, rows[:, half:], rows[:, :half])

    def cut(rows, j):
        return rows[:, j * WIDTH : (j + 1) * WIDTH]

    def shared(mine, other):
        return mine, lax.ppermute(other, "tok", swap)

    query_halves = own_half(query_rows), other_half(query_rows)
    key_rows, value_rows = after((key_rows, value_rows), query_halves)
    query = shared(*query_halves)
    key = shared(own_half(key_rows), other_half(key_rows))
    value = shared(own_half(value_rows), other_half(value_rows))
    first = chip * 2 * block
    bases = [first + core * block, first + (1 - core) * block]
    meta = jnp.stack(
        bases
        + [b - 2 * block for b in bases]
        + [(chip == 1) | (chip == 2), chip == 1, chip >= 0, chip == 1, chip >= 2, chip == 3]
    ).astype(jnp.int32)
    rows_out = 2 * block + STAT_ROWS
    flops = 4 * 512 * 512 * 224 * 4 * 2
    queries, keys, keys_before, one, two, mine, other = ([] for _ in range(7))
    spare = jnp.zeros((STAT_ROWS, WIDTH), query_rows.dtype)
    for j in range(chunks):
        queries.append(jnp.concatenate([cut(query[0], j), cut(query[1], j), spare], axis=0))
        keys.append(jnp.concatenate([cut(key[0], j), cut(key[1], j), cut(value[0], j), cut(value[1], j)], axis=0))

    def between(array, *moves):
        return lax.ppermute(array, "tok", [(2 * a + i, 2 * b + i) for a, b in moves for i in range(2)])

    def ahead(j, *given):
        return call(
            remote_kernel, count, block, [(rows_out, WIDTH)] * 2,
            [meta, ends, one[j], two[j], keys[j], keys_before[j], *given], flops,
        )

    def phase(payloads, moves_one, moves_two, given=None, earlier=()):
        number = len(one)
        sent = payloads + ((keys[number],) if number < chunks else ())
        if number > 0:
            sent = after(sent, (one[-1], two[-1], *keys_before[number - 1 : chunks - 1][:1], *earlier))
        one.append(between(sent[0], *moves_one))
        two.append(between(sent[1], *moves_two))
        if number < chunks:
            keys_before.append(between(sent[2], (0, 1)))
        return None if given is None else tuple(ahead(number - 1, *given))

    def home(j):
        out_mine, out_other = call(
            home_kernel, count, block, [(block, WIDTH)] * 2,
            [meta, ends, queries[j], keys[j], keys_before[j], two[j + 2], one[j + 2]], flops,
        )
        mine.append(out_mine)
        other.append(out_other)

    full = ((2, 1), (3, 2), (1, 3)), ((3, 1), (1, 2), (2, 3))
    back = ((1, 3),), ((1, 2), (2, 3))
    phase((queries[0], queries[0]), ((2, 1), (3, 2)), ((3, 1),))
    cache = CacheMoves(cache_blocks, targets, queries[0])
    parts_two = phase((queries[1], queries[1]), ((2, 1), (3, 2)), ((3, 1),), given=(queries[2],))
    early_one = between(cache.raw(chip + 1), (1, 2), (2, 3))
    early_two = between(cache.raw(chip + 2), (1, 3))
    early_three, early_four = after((cache.raw(2), cache.raw(3)), (one[0], keys_before[0], early_one, early_two))
    early_three, early_four = between(early_three, (0, 2)), between(early_four, (0, 3))
    parts_three = phase(parts_two, *full, given=(queries[3],), earlier=(cache.grouped,))
    parts_four = phase(parts_three, *full, given=())
    earlier = (one[2], two[2], keys_before[2])
    apart_two = between(after((cache.piece(2),), earlier)[0], (2, 0), (3, 1))
    apart_three = between(after((cache.piece(3),), earlier)[0], (3, 0), (2, 1))
    home(0)
    parts_five = phase(parts_four, *back, given=(), earlier=(mine[0], early_one, early_two, early_three, early_four))
    cache.collect(after((early_one, early_two, jnp.where(chip == 2, early_three, early_four)), (one[3], two[3])))
    home(1)
    parts_five = after(parts_five, (apart_two,))
    one.append(between(parts_five[0], *back[0]))
    two.append(between(parts_five[1], *back[1]))
    apart_one = between(after((cache.piece(1),), (one[4],))[0], (0, 1), (1, 0), (3, 2))
    home(2)
    cache.prepare(apart_one, apart_two, apart_three)
    queries[3] = after((queries[3],), (cache.sent,))[0]
    home(3)
    moved_cache = cache.result()
    others = [lax.ppermute(jnp.concatenate(other[:-1], axis=1), "tok", swap), lax.ppermute(other[-1], "tok", swap)]
    mine, other = jnp.concatenate(mine, axis=1), jnp.concatenate(others, axis=1)
    attended = jnp.concatenate([jnp.where(core == 0, mine, other), jnp.where(core == 0, other, mine)], axis=1)
    return attended, moved_cache


def assemble_kernel(places_ref, here_ref, one_ref, two_ref, three_ref, early_ref, partner_ref, out_ref):
    core = places_ref[0]
    for i, piece_ref in enumerate((here_ref, one_ref, two_ref, three_ref)):
        chip, early = places_ref[1 + i], places_ref[5 + i]
        out_ref[:, pl.ds(2 * chip + 1 - core, 1)] = partner_ref[:, i : i + 1]

        @pl.when(early > 0)
        def _(i=i, chip=chip):
            out_ref[:, pl.ds(2 * chip + core, 1)] = early_ref[:, places_ref[9 + i], pl.ds(core, 1)]

        @pl.when(early == 0)
        def _(piece_ref=piece_ref, chip=chip):
            out_ref[:, pl.ds(2 * chip + core, 1)] = piece_ref[:, pl.ds(core, 1)]


class CacheMoves:
    def __init__(self, cache_blocks, targets, earlier):
        self.groups = lax.axis_size("req")
        index = lax.axis_index("tok")
        self.chip, self.core = index // 2, index % 2
        (cache_blocks, targets) = after((cache_blocks, targets), (earlier,))
        placing = slots_of(targets, self.groups, cache_blocks.dtype)
        block_count, kinds, heads, entries = cache_blocks.shape
        local = cache_blocks.reshape(block_count, kinds, 4, 2, heads // 8, entries)
        outgoing = jnp.einsum("bdc,bjtkhy->dtcjkhy", placing, local, preferred_element_type=jnp.float32)
        self.outgoing = outgoing.astype(jnp.bfloat16)
        self.grouped = lax.all_to_all(self.outgoing, "req", split_axis=0, concat_axis=0, tiled=True)
        self.flat = (self.groups * CAP * kinds, 2, heads // 8, entries)

    def raw(self, chip):
        return lax.dynamic_index_in_dim(self.outgoing, jnp.clip(chip, 0, 3), axis=1, keepdims=False)

    def piece(self, distance):
        return lax.dynamic_index_in_dim(self.grouped, self.chip ^ distance, axis=1, keepdims=False)

    def collect(self, pieces):
        both = jnp.stack(pieces, axis=1)
        self.arrived = lax.all_to_all(both, "req", split_axis=0, concat_axis=0, tiled=True)

    def prepare(self, *apart):
        shape = self.flat
        chip = self.chip
        self.pieces = [p.reshape(shape) for p in (self.piece(0), *apart)]
        arrived = self.arrived.reshape((self.groups, 3, -1) + shape[1:])
        self.early_pieces = jnp.transpose(arrived, (0, 2, 1, 3, 4, 5)).reshape((shape[0], 3) + shape[1:])
        self.early = [chip < 0, chip == 3, chip >= 2, chip >= 2]
        self.which = [0, 0, jnp.where(chip == 2, 2, 1), jnp.where(chip == 2, 0, 2)]
        sent = []
        for i, piece in enumerate(self.pieces):
            if i > 0:
                instead = lax.dynamic_index_in_dim(self.early_pieces, self.which[i], axis=1, keepdims=False)
                piece = jnp.where(self.early[i], instead, piece)
            sent.append(jnp.where(self.core == 0, piece[:, 1], piece[:, 0]))
        self.sent = jnp.stack(sent, axis=1)

    def result(self):
        shape, chip, core = self.flat, self.chip, self.core
        pieces, arrived, early, which = self.pieces, self.early_pieces, self.early, self.which
        partner = lax.ppermute(self.sent, "tok", [(i, i ^ 1) for i in range(8)])
        places = jnp.stack([core] + [chip ^ d for d in range(4)] + early + which).astype(jnp.int32)
        step = 2

        def blocks(array):
            return pl.BlockSpec((step,) + array.shape[1:], lambda i: (i,) + (0,) * (array.ndim - 1))

        arrays = (*pieces, arrived, partner)
        out = jax.ShapeDtypeStruct((shape[0], 8) + shape[2:], jnp.bfloat16)
        out = pl.pallas_call(
            assemble_kernel,
            out_shape=out,
            grid=(shape[0] // step,),
            in_specs=[pl.BlockSpec(memory_space=pltpu.SMEM)] + [blocks(array) for array in arrays],
            out_specs=blocks(out),
            compiler_params=pltpu.CompilerParams(vmem_limit_bytes=40 * 1024 * 1024),
        )(places, *arrays)
        return out.reshape((self.groups, CAP, -1) + out.shape[1:])


def attend_heads_all(query_rows, key_rows, value_rows, lengths):
    tok_count = lax.axis_size("tok")
    rows, feature = query_rows.shape
    group = feature // tok_count
    length = rows * tok_count

    def regroup(array):
        return lax.all_to_all(array, "tok", split_axis=1, concat_axis=0, tiled=True)

    query, key, value = regroup(query_rows), regroup(key_rows), regroup(value_rows)
    ends = jnp.cumsum(lengths)
    position = jnp.arange(length, dtype=jnp.int32)
    segments = jnp.sum((position[:, None] >= ends[None, :]).astype(jnp.int32), axis=1)
    block = min(512, length)
    blocks = []
    for low in range(0, length, block):
        high = low + block
        visible = (segments[low:high, None] == segments[None, :high]) & (position[low:high, None] >= position[None, :high])
        heads = []
        for head in range(group // HD):
            lanes = slice(head * HD, (head + 1) * HD)
            scores = lax.dot_general(
                query[low:high, lanes], key[:high, lanes], (((1,), (1,)), ((), ())), preferred_element_type=jnp.float32
            )
            scores = jnp.where(visible, scores * HD**-0.5, NEG)
            weights = jnp.where(visible, jnp.exp(scores - jnp.max(scores, axis=1, keepdims=True)), 0.0)
            total = jnp.sum(weights, axis=1, keepdims=True)
            summed = jnp.dot(weights.astype(jnp.bfloat16), value[:high, lanes], preferred_element_type=jnp.float32)
            heads.append((summed / total).astype(jnp.bfloat16))
        blocks.append(jnp.concatenate(heads, axis=1))
    return lax.all_to_all(jnp.concatenate(blocks, axis=0), "tok", split_axis=0, concat_axis=1, tiled=True)


def slots_of(targets, groups, dtype):
    positions = jnp.arange(targets.shape[0], dtype=jnp.int32)
    earlier = (targets[:, None] == targets[None, :]) & (positions[None, :] < positions[:, None])
    slot_rank = jnp.sum(earlier.astype(jnp.int32), axis=1)
    return (
        (targets[:, None, None] == jnp.arange(groups, dtype=jnp.int32)[None, :, None])
        & (slot_rank[:, None, None] == jnp.arange(CAP, dtype=jnp.int32)[None, None, :])
    ).astype(dtype)


def relocate(cache_blocks, targets):
    groups = lax.axis_size("req")
    tok_count = lax.axis_size("tok")
    block_count, kinds, heads, entries = cache_blocks.shape
    placing = slots_of(targets, groups, cache_blocks.dtype)
    here = heads // tok_count
    local = cache_blocks.reshape(block_count, kinds, tok_count, here, entries)
    outgoing = jnp.einsum("bdc,bjthy->dtcjhy", placing, local, preferred_element_type=jnp.float32).astype(jnp.bfloat16)
    outgoing = outgoing.reshape(groups * tok_count, CAP, kinds, here, entries)
    arrived = lax.all_to_all(outgoing, ("req", "tok"), split_axis=0, concat_axis=0, tiled=True)
    arrived = arrived.reshape(groups, tok_count, CAP, kinds, here, entries)
    return jnp.transpose(arrived, (0, 2, 3, 1, 4, 5))


def on_device(query_rows, key_rows, value_rows, lengths, cache_blocks, destinations):
    targets = destinations[0, :, 0]
    if lax.axis_size("tok") == 8:
        attended, moved_cache = attend_chips(
            query_rows[0], key_rows[0], value_rows[0], lengths[0], cache_blocks[0], targets
        )
    else:
        attended = attend_heads_all(query_rows[0], key_rows[0], value_rows[0], lengths[0])
        moved_cache = relocate(cache_blocks[0], targets)
    return (attended[None], moved_cache[None])


def solution(mesh):
    return jax.shard_map(
        on_device,
        mesh=mesh,
        in_specs=(
            P("req", "tok", None),
            P("req", "tok", None),
            P("req", "tok", None),
            P("req", None),
            P("req", "tok", None, None, None),
            P("req", "tok", None),
        ),
        out_specs=(P("req", "tok", None), P("req", None, None, None, None, "tok", None)),
        check_vma=False,
    )
```

```python
import functools
import math

import jax
import jax.numpy as jnp
from jax import lax
from jax.experimental import pallas as pl
from jax.experimental.pallas import tpu as pltpu
from jax.sharding import PartitionSpec as P

HD = 224
CAP = 2
GROUP = 4
WIDTH = GROUP * HD
NEG = -1e30
FLOOR = -1e29
EXP2_SCALE = HD**-0.5 * math.log2(math.e)
STAT_ROWS = 16
TILE = 32
WINDOWS = tuple((h * HD // 128 * 128, -(-(h + 1) * HD // 128) * 128) for h in range(GROUP))


def starts_of(ends_ref, count, position):
    start = jnp.zeros_like(position)
    for i in range(count):
        end = ends_ref[i]
        start = jnp.where(position >= end, end, start)
    return start


def lanes_of(head, rows):
    low, high = WINDOWS[head]
    lane = lax.broadcasted_iota(jnp.int32, (rows, high - low), 1) + low
    return (lane >= head * HD) & (lane < (head + 1) * HD)


def attend_block(ends_ref, count, query_ref, row, base, key_refs, m_ref, l_ref, acc_ref, work):
    scores_ref, weights_ref, hidden_ref, decay_ref = work
    rows = m_ref.shape[1]
    lowest = starts_of(ends_ref, count, base)
    m_ref[...] = jnp.full(m_ref.shape, FLOOR, jnp.float32)
    l_ref[...] = jnp.zeros(l_ref.shape, jnp.float32)
    acc_ref[...] = jnp.zeros(acc_ref.shape, jnp.float32)
    for key_ref, bases, usable in key_refs:
        depth = key_ref.shape[0] // 2
        begin = jnp.minimum(bases[0], bases[1])
        needed = usable & (lowest < begin + depth) & (base + rows > begin)

        @pl.when(needed)
        def _(key_ref=key_ref, bases=bases, depth=depth):
            column = lax.broadcasted_iota(jnp.int32, (1, depth), 1)
            key_position = jnp.where(column < depth // 2, bases[0] + column, bases[1] + column - depth // 2)
            for tile in range(0, rows, TILE):
                position = base + tile + lax.broadcasted_iota(jnp.int32, (TILE, 1), 0)
                first = starts_of(ends_ref, count, position)
                visible = (key_position <= position) & (key_position >= first)
                hidden_ref[tile : tile + TILE] = jnp.where(visible, 0.0, NEG)
            for head in range(GROUP):
                low, high = WINDOWS[head]
                query = query_ref[pl.ds(row, rows), low:high]
                query = jnp.where(lanes_of(head, rows), query, jnp.zeros((), query.dtype))
                scores_ref[head] = lax.dot_general(
                    query, key_ref[:depth, low:high], (((1,), (1,)), ((), ())), preferred_element_type=jnp.float32
                )
            for head in range(GROUP):
                low, high = WINDOWS[head]
                for tile in range(0, rows, TILE):
                    part = slice(tile, tile + TILE)
                    scores = scores_ref[head, part] + hidden_ref[part]
                    old = m_ref[head, part]
                    new = jnp.maximum(old, jnp.max(scores, axis=1, keepdims=True))
                    weights = jnp.exp2((scores - new[:, :1]) * EXP2_SCALE)
                    decay = jnp.exp2((old - new) * EXP2_SCALE)
                    m_ref[head, part] = new
                    decay_ref[head, part] = decay
                    l_ref[head, part] = l_ref[head, part] * decay + jnp.sum(weights, axis=1, keepdims=True)
                    weights_ref[head, part] = weights.astype(jnp.bfloat16)
                summed = jnp.dot(weights_ref[head], key_ref[depth:, low:high], preferred_element_type=jnp.float32)
                for lane in range(0, high - low, 128):
                    lanes = slice(lane, lane + 128)
                    acc_ref[head, :, lanes] = acc_ref[head, :, lanes] * decay_ref[head] + summed[:, lanes]


def place(out_ref, row, rows, head, value, scratch_ref):
    low, high = WINDOWS[head]
    lane = lax.broadcasted_iota(jnp.int32, (rows, high - low), 1) + low
    if head > 0:
        value = jnp.where(lane >= head * HD, value, scratch_ref[:, low:high])
    scratch_ref[:, low:high] = value
    if head == GROUP - 1:
        out_ref[pl.ds(row, rows), :] = scratch_ref[...].astype(out_ref.dtype)


def remote_kernel(
    count, block, meta_ref, ends_ref, near_ref, far_ref, own_ref, prev_ref, *refs
):
    spare, (one_out, two_out, m_ref, l_ref, acc_ref, row_ref, *work) = refs[:-10], refs[-10:]
    own = (own_ref, (meta_ref[0], meta_ref[1]), meta_ref[6] > 0)
    prev = (prev_ref, (meta_ref[2], meta_ref[3]), meta_ref[7] > 0)
    depth = own_ref.shape[0] // 2
    for query_ref, out_ref, hops, enabled in ((near_ref, two_out, 1, meta_ref[4]), (far_ref, one_out, 2, meta_ref[5])):
        if spare:

            @pl.when(enabled == 0)
            def _(out_ref=out_ref):
                out_ref[...] = spare[0][...]

        @pl.when(enabled > 0)
        def _(query_ref=query_ref, out_ref=out_ref, hops=hops):
            @pl.loop(0, 2)
            def _(i):
                row = pl.multiple_of(i * block, block)
                base = jnp.where(i == 0, meta_ref[0], meta_ref[1]) + hops * depth
                attend_block(ends_ref, count, query_ref, row, base, (own, prev), m_ref, l_ref, acc_ref, work)
                lane = lax.broadcasted_iota(jnp.int32, (block, 128), 1)
                stats = jnp.zeros((block, 128), jnp.float32)
                for head in range(GROUP):
                    low, high = WINDOWS[head]
                    total = l_ref[head][:, :1]
                    empty = total == 0.0
                    safe = jnp.where(empty, 1.0, total)
                    place(out_ref, row, block, head, acc_ref[head, :, : high - low] / safe, row_ref)
                    level = jnp.where(empty, NEG, m_ref[head][:, :1] * EXP2_SCALE + jnp.log2(safe))
                    for part in range(3):
                        piece = level.astype(jnp.bfloat16).astype(jnp.float32)
                        stats = jnp.where(lane == part * GROUP + head, piece, stats)
                        level = level - piece
                flat = jnp.transpose(stats)[:STAT_ROWS].astype(jnp.bfloat16)
                out_ref[2 * block :, pl.ds(row, block)] = flat


def local_kernel(
    count, block, meta_ref, ends_ref, query_ref, own_ref, prev_ref, value_out, level_out, m_ref, l_ref, acc_ref, row_ref, *work
):
    own = (own_ref, (meta_ref[0], meta_ref[1]), meta_ref[6] > 0)
    prev = (prev_ref, (meta_ref[2], meta_ref[3]), meta_ref[7] > 0)

    @pl.loop(0, 2)
    def _(i):
        row = pl.multiple_of(i * block, block)
        base = jnp.where(i == 0, meta_ref[0], meta_ref[1])
        attend_block(ends_ref, count, query_ref, row, base, (own, prev), m_ref, l_ref, acc_ref, work)
        lane = lax.broadcasted_iota(jnp.int32, (block, 128), 1)
        levels = jnp.zeros((block, 128), jnp.float32)
        for head in range(GROUP):
            low, high = WINDOWS[head]
            total = l_ref[head][:, :1]
            levels = jnp.where(lane == head, m_ref[head][:, :1] * EXP2_SCALE + jnp.log2(total), levels)
            place(value_out, row, block, head, acc_ref[head, :, : high - low] / total, row_ref)
        level_out[pl.ds(row, block), :] = levels


def merge_kernel(count, block, meta_ref, ends_ref, value_ref, level_ref, near_ref, far_ref, mine_out, other_out, row_ref):
    for i, out_ref in enumerate((mine_out, other_out)):
        row = i * block
        parts = []
        for part_ref, enabled in ((near_ref, meta_ref[8]), (far_ref, meta_ref[9])):
            stats = jnp.transpose(part_ref[2 * block :, row : row + block].astype(jnp.float32))
            parts.append((part_ref, stats, enabled > 0))
        for head in range(GROUP):
            low, high = WINDOWS[head]
            level = level_ref[row : row + block, head : head + 1]
            others = []
            for part_ref, stats, enabled in parts:
                theirs = stats[:, head : head + 1] + stats[:, GROUP + head : GROUP + head + 1]
                theirs = theirs + stats[:, 2 * GROUP + head : 2 * GROUP + head + 1]
                others.append((part_ref, jnp.where(enabled, theirs, NEG)))
            top = jnp.maximum(jnp.maximum(level, others[0][1]), others[1][1])
            total = jnp.exp2(level - top)
            value = value_ref[row : row + block, low:high] * total
            for part_ref, theirs in others:
                weight = jnp.exp2(theirs - top)
                total = total + weight
                value = value + part_ref[row : row + block, low:high].astype(jnp.float32) * weight
            place(out_ref, 0, block, head, value / total, row_ref)


def home_kernel(
    count, block, meta_ref, ends_ref, query_ref, own_ref, prev_ref, near_ref, far_ref, mine_out, other_out, m_ref, l_ref, acc_ref, row_ref, *work
):
    own = (own_ref, (meta_ref[0], meta_ref[1]), meta_ref[6] > 0)
    prev = (prev_ref, (meta_ref[2], meta_ref[3]), meta_ref[7] > 0)
    for i, out_ref in enumerate((mine_out, other_out)):
        row = i * block
        attend_block(ends_ref, count, query_ref, row, meta_ref[i], (own, prev), m_ref, l_ref, acc_ref, work)
        parts = []
        for part_ref, enabled in ((near_ref, meta_ref[8]), (far_ref, meta_ref[9])):
            stats = jnp.transpose(part_ref[2 * block :, row : row + block].astype(jnp.float32))
            parts.append((part_ref, stats, enabled > 0))
        for head in range(GROUP):
            low, high = WINDOWS[head]
            level = m_ref[head][:, :1] * EXP2_SCALE
            others = []
            for part_ref, stats, enabled in parts:
                theirs = stats[:, head : head + 1] + stats[:, GROUP + head : GROUP + head + 1]
                theirs = theirs + stats[:, 2 * GROUP + head : 2 * GROUP + head + 1]
                others.append((part_ref, jnp.where(enabled, theirs, NEG)))
            top = jnp.maximum(jnp.maximum(level, others[0][1]), others[1][1])
            weight = jnp.exp2(level - top)
            total = l_ref[head][:, :1] * weight
            value = acc_ref[head, :, : high - low] * weight
            for part_ref, theirs in others:
                weight = jnp.exp2(theirs - top)
                total = total + weight
                value = value + part_ref[row : row + block, low:high].astype(jnp.float32) * weight
            place(out_ref, 0, block, head, value / total, row_ref)


def scratch(block):
    widest = max(high - low for low, high in WINDOWS)
    return [
        pltpu.VMEM((GROUP, block, 128), jnp.float32),
        pltpu.VMEM((GROUP, block, 128), jnp.float32),
        pltpu.VMEM((GROUP, block, widest), jnp.float32),
        pltpu.VMEM((block, WIDTH), jnp.float32),
        pltpu.VMEM((GROUP, block, 2 * block), jnp.float32),
        pltpu.VMEM((GROUP, block, 2 * block), jnp.bfloat16),
        pltpu.VMEM((block, 2 * block), jnp.float32),
        pltpu.VMEM((GROUP, block, 128), jnp.float32),
    ]


def call(kernel, count, block, outs, arrays, flops, scratch_shapes=None):
    smem = pl.BlockSpec(memory_space=pltpu.SMEM)
    vmem = pl.BlockSpec(memory_space=pltpu.VMEM)
    return pl.pallas_call(
        functools.partial(kernel, count, block),
        out_shape=[out if hasattr(out, 'dtype') else jax.ShapeDtypeStruct(out, jnp.bfloat16) for out in outs],
        in_specs=[smem, smem] + [vmem] * (len(arrays) - 2),
        out_specs=[vmem] * len(outs),
        scratch_shapes=scratch_shapes or scratch(block),
        compiler_params=pltpu.CompilerParams(vmem_limit_bytes=40 * 1024 * 1024),
        cost_estimate=pl.CostEstimate(flops=flops, bytes_accessed=8 * 1024 * 1024, transcendentals=flops // 1000),
    )(*arrays)


def after(arrays, earlier):
    return lax.optimization_barrier((tuple(arrays), tuple(earlier)))[0]


def attend_chips(query_rows, key_rows, value_rows, lengths, cache_blocks, targets):
    index = lax.axis_index("tok")
    core = index % 2
    chip = index // 2
    block, feature = query_rows.shape
    half = feature // 2
    chunks = half // WIDTH
    count = lengths.shape[0]
    ends = jnp.cumsum(lengths).astype(jnp.int32)
    swap = [(i, i ^ 1) for i in range(8)]

    def own_half(rows):
        return jnp.where(core == 0, rows[:, :half], rows[:, half:])

    def other_half(rows):
        return jnp.where(core == 0, rows[:, half:], rows[:, :half])

    def cut(rows, j):
        return rows[:, j * WIDTH : (j + 1) * WIDTH]

    def shared(mine, other):
        return mine, lax.ppermute(other, "tok", swap)

    query_halves = own_half(query_rows), other_half(query_rows)
    key_rows, value_rows = after((key_rows, value_rows), query_halves)
    query = shared(*query_halves)
    key = shared(own_half(key_rows), other_half(key_rows))
    value = shared(own_half(value_rows), other_half(value_rows))
    first = chip * 2 * block
    bases = [first + core * block, first + (1 - core) * block]
    meta = jnp.stack(
        bases
        + [b - 2 * block for b in bases]
        + [(chip == 1) | (chip == 2), chip == 1, chip >= 0, chip == 1, chip >= 2, chip == 3]
    ).astype(jnp.int32)
    rows_out = 2 * block + STAT_ROWS
    flops = 4 * 512 * 512 * 224 * 4 * 2
    queries, keys, keys_before, one, two, mine, other = ([] for _ in range(7))
    spare = jnp.zeros((STAT_ROWS, WIDTH), query_rows.dtype)
    for j in range(chunks):
        queries.append(jnp.concatenate([cut(query[0], j), cut(query[1], j), spare], axis=0))
        keys.append(jnp.concatenate([cut(key[0], j), cut(key[1], j), cut(value[0], j), cut(value[1], j)], axis=0))

    def between(array, *moves):
        return lax.ppermute(array, "tok", [(2 * a + i, 2 * b + i) for a, b in moves for i in range(2)])

    def ahead(j, *given):
        return call(
            remote_kernel, count, block, [(rows_out, WIDTH)] * 2,
            [meta, ends, one[j], two[j], keys[j], keys_before[j], *given], flops,
        )

    def phase(payloads, moves_one, moves_two, given=None, earlier=()):
        number = len(one)
        sent = payloads + ((keys[number],) if number < chunks else ())
        if number > 0:
            sent = after(sent, (one[-1], two[-1], *keys_before[number - 1 : chunks - 1][:1], *earlier))
        one.append(between(sent[0], *moves_one))
        two.append(between(sent[1], *moves_two))
        if number < chunks:
            keys_before.append(between(sent[2], (0, 1)))
        return None if given is None else tuple(ahead(number - 1, *given))

    def home(j):
        if j < chunks - 1:
            out_mine, out_other = call(
                home_kernel, count, block, [(block, WIDTH)] * 2,
                [meta, ends, queries[j], keys[j], keys_before[j], two[j + 2], one[j + 2]], flops,
            )
        else:
            value, level = call(
                local_kernel, count, block,
                [jax.ShapeDtypeStruct((2 * block, lanes), jnp.float32) for lanes in (WIDTH, 128)],
                [meta, ends, queries[j], keys[j], keys_before[j]], flops,
            )
            out_mine, out_other = call(
                merge_kernel, count, block, [(block, WIDTH)] * 2,
                [meta, ends, value, level, two[j + 2], one[j + 2]], flops // 16, [pltpu.VMEM((block, WIDTH), jnp.float32)],
            )
        mine.append(out_mine)
        other.append(out_other)

    full = ((2, 1), (3, 2), (1, 3)), ((3, 1), (1, 2), (2, 3))
    back = ((1, 3),), ((1, 2), (2, 3))
    phase((queries[0], queries[0]), ((2, 1), (3, 2)), ((3, 1),))
    cache = CacheMoves(cache_blocks, targets, queries[0])
    parts_two = phase((queries[1], queries[1]), ((2, 1), (3, 2)), ((3, 1),), given=(queries[2],))
    early_one = between(cache.raw(chip + 1), (1, 2), (2, 3))
    early_two = between(cache.raw(chip + 2), (1, 3))
    early_three, early_four = after((cache.raw(2), cache.raw(3)), (one[0], keys_before[0], early_one, early_two))
    early_three, early_four = between(early_three, (0, 2)), between(early_four, (0, 3))
    parts_three = phase(parts_two, *full, given=(queries[3],), earlier=(cache.grouped,))
    parts_four = phase(parts_three, *full, given=())
    earlier = (one[2], two[2], keys_before[2])
    apart_two = between(after((cache.piece(2),), earlier)[0], (2, 0), (3, 1))
    apart_three = between(after((cache.piece(3),), earlier)[0], (3, 0), (2, 1))
    home(0)
    parts_five = phase(parts_four, *back, given=(), earlier=(mine[0], early_one, early_two, early_three, early_four))
    cache.collect(after((early_one, early_two, jnp.where(chip == 2, early_three, early_four)), (one[3], two[3])))
    home(1)
    parts_five = after(parts_five, (apart_two,))
    one.append(between(parts_five[0], *back[0]))
    two.append(between(parts_five[1], *back[1]))
    apart_one = between(after((cache.piece(1),), (one[4],))[0], (0, 1), (1, 0), (3, 2))
    home(2)
    cache.prepare(apart_one, apart_two, apart_three)
    queries[3] = after((queries[3],), (cache.sent,))[0]
    home(3)
    moved_cache = cache.result()
    others = [lax.ppermute(jnp.concatenate(other[:-1], axis=1), "tok", swap), lax.ppermute(other[-1], "tok", swap)]
    mine, other = jnp.concatenate(mine, axis=1), jnp.concatenate(others, axis=1)
    attended = jnp.concatenate([jnp.where(core == 0, mine, other), jnp.where(core == 0, other, mine)], axis=1)
    return attended, moved_cache


def assemble_kernel(places_ref, here_ref, one_ref, two_ref, three_ref, early_ref, partner_ref, out_ref):
    core = places_ref[0]
    for i, piece_ref in enumerate((here_ref, one_ref, two_ref, three_ref)):
        chip, early = places_ref[1 + i], places_ref[5 + i]
        out_ref[:, pl.ds(2 * chip + 1 - core, 1)] = partner_ref[:, i : i + 1]

        @pl.when(early > 0)
        def _(i=i, chip=chip):
            out_ref[:, pl.ds(2 * chip + core, 1)] = early_ref[:, places_ref[9 + i], pl.ds(core, 1)]

        @pl.when(early == 0)
        def _(piece_ref=piece_ref, chip=chip):
            out_ref[:, pl.ds(2 * chip + core, 1)] = piece_ref[:, pl.ds(core, 1)]


class CacheMoves:
    def __init__(self, cache_blocks, targets, earlier):
        self.groups = lax.axis_size("req")
        index = lax.axis_index("tok")
        self.chip, self.core = index // 2, index % 2
        (cache_blocks, targets) = after((cache_blocks, targets), (earlier,))
        placing = slots_of(targets, self.groups, cache_blocks.dtype)
        block_count, kinds, heads, entries = cache_blocks.shape
        local = cache_blocks.reshape(block_count, kinds, 4, 2, heads // 8, entries)
        outgoing = jnp.einsum("bdc,bjtkhy->dtcjkhy", placing, local, preferred_element_type=jnp.float32)
        self.outgoing = outgoing.astype(jnp.bfloat16)
        self.grouped = lax.all_to_all(self.outgoing, "req", split_axis=0, concat_axis=0, tiled=True)
        self.flat = (self.groups * CAP * kinds, 2, heads // 8, entries)

    def raw(self, chip):
        return lax.dynamic_index_in_dim(self.outgoing, jnp.clip(chip, 0, 3), axis=1, keepdims=False)

    def piece(self, distance):
        return lax.dynamic_index_in_dim(self.grouped, self.chip ^ distance, axis=1, keepdims=False)

    def collect(self, pieces):
        both = jnp.stack(pieces, axis=1)
        self.arrived = lax.all_to_all(both, "req", split_axis=0, concat_axis=0, tiled=True)

    def prepare(self, *apart):
        shape = self.flat
        chip = self.chip
        self.pieces = [p.reshape(shape) for p in (self.piece(0), *apart)]
        arrived = self.arrived.reshape((self.groups, 3, -1) + shape[1:])
        self.early_pieces = jnp.transpose(arrived, (0, 2, 1, 3, 4, 5)).reshape((shape[0], 3) + shape[1:])
        self.early = [chip < 0, chip == 3, chip >= 2, chip >= 2]
        self.which = [0, 0, jnp.where(chip == 2, 2, 1), jnp.where(chip == 2, 0, 2)]
        sent = []
        for i, piece in enumerate(self.pieces):
            if i > 0:
                instead = lax.dynamic_index_in_dim(self.early_pieces, self.which[i], axis=1, keepdims=False)
                piece = jnp.where(self.early[i], instead, piece)
            sent.append(jnp.where(self.core == 0, piece[:, 1], piece[:, 0]))
        self.sent = jnp.stack(sent, axis=1)

    def result(self):
        shape, chip, core = self.flat, self.chip, self.core
        pieces, arrived, early, which = self.pieces, self.early_pieces, self.early, self.which
        partner = lax.ppermute(self.sent, "tok", [(i, i ^ 1) for i in range(8)])
        places = jnp.stack([core] + [chip ^ d for d in range(4)] + early + which).astype(jnp.int32)
        step = 2

        def blocks(array):
            return pl.BlockSpec((step,) + array.shape[1:], lambda i: (i,) + (0,) * (array.ndim - 1))

        arrays = (*pieces, arrived, partner)
        out = jax.ShapeDtypeStruct((shape[0], 8) + shape[2:], jnp.bfloat16)
        out = pl.pallas_call(
            assemble_kernel,
            out_shape=out,
            grid=(shape[0] // step,),
            in_specs=[pl.BlockSpec(memory_space=pltpu.SMEM)] + [blocks(array) for array in arrays],
            out_specs=blocks(out),
            compiler_params=pltpu.CompilerParams(vmem_limit_bytes=40 * 1024 * 1024),
        )(places, *arrays)
        return out.reshape((self.groups, CAP, -1) + out.shape[1:])


def attend_heads_all(query_rows, key_rows, value_rows, lengths):
    tok_count = lax.axis_size("tok")
    rows, feature = query_rows.shape
    group = feature // tok_count
    length = rows * tok_count

    def regroup(array):
        return lax.all_to_all(array, "tok", split_axis=1, concat_axis=0, tiled=True)

    query, key, value = regroup(query_rows), regroup(key_rows), regroup(value_rows)
    ends = jnp.cumsum(lengths)
    position = jnp.arange(length, dtype=jnp.int32)
    segments = jnp.sum((position[:, None] >= ends[None, :]).astype(jnp.int32), axis=1)
    block = min(512, length)
    blocks = []
    for low in range(0, length, block):
        high = low + block
        visible = (segments[low:high, None] == segments[None, :high]) & (position[low:high, None] >= position[None, :high])
        heads = []
        for head in range(group // HD):
            lanes = slice(head * HD, (head + 1) * HD)
            scores = lax.dot_general(
                query[low:high, lanes], key[:high, lanes], (((1,), (1,)), ((), ())), preferred_element_type=jnp.float32
            )
            scores = jnp.where(visible, scores * HD**-0.5, NEG)
            weights = jnp.where(visible, jnp.exp(scores - jnp.max(scores, axis=1, keepdims=True)), 0.0)
            total = jnp.sum(weights, axis=1, keepdims=True)
            summed = jnp.dot(weights.astype(jnp.bfloat16), value[:high, lanes], preferred_element_type=jnp.float32)
            heads.append((summed / total).astype(jnp.bfloat16))
        blocks.append(jnp.concatenate(heads, axis=1))
    return lax.all_to_all(jnp.concatenate(blocks, axis=0), "tok", split_axis=0, concat_axis=1, tiled=True)


def slots_of(targets, groups, dtype):
    positions = jnp.arange(targets.shape[0], dtype=jnp.int32)
    earlier = (targets[:, None] == targets[None, :]) & (positions[None, :] < positions[:, None])
    slot_rank = jnp.sum(earlier.astype(jnp.int32), axis=1)
    return (
        (targets[:, None, None] == jnp.arange(groups, dtype=jnp.int32)[None, :, None])
        & (slot_rank[:, None, None] == jnp.arange(CAP, dtype=jnp.int32)[None, None, :])
    ).astype(dtype)


def relocate(cache_blocks, targets):
    groups = lax.axis_size("req")
    tok_count = lax.axis_size("tok")
    block_count, kinds, heads, entries = cache_blocks.shape
    placing = slots_of(targets, groups, cache_blocks.dtype)
    here = heads // tok_count
    local = cache_blocks.reshape(block_count, kinds, tok_count, here, entries)
    outgoing = jnp.einsum("bdc,bjthy->dtcjhy", placing, local, preferred_element_type=jnp.float32).astype(jnp.bfloat16)
    outgoing = outgoing.reshape(groups * tok_count, CAP, kinds, here, entries)
    arrived = lax.all_to_all(outgoing, ("req", "tok"), split_axis=0, concat_axis=0, tiled=True)
    arrived = arrived.reshape(groups, tok_count, CAP, kinds, here, entries)
    return jnp.transpose(arrived, (0, 2, 3, 1, 4, 5))


def on_device(query_rows, key_rows, value_rows, lengths, cache_blocks, destinations):
    targets = destinations[0, :, 0]
    if lax.axis_size("tok") == 8:
        attended, moved_cache = attend_chips(
            query_rows[0], key_rows[0], value_rows[0], lengths[0], cache_blocks[0], targets
        )
    else:
        attended = attend_heads_all(query_rows[0], key_rows[0], value_rows[0], lengths[0])
        moved_cache = relocate(cache_blocks[0], targets)
    return (attended[None], moved_cache[None])


def solution(mesh):
    return jax.shard_map(
        on_device,
        mesh=mesh,
        in_specs=(
            P("req", "tok", None),
            P("req", "tok", None),
            P("req", "tok", None),
            P("req", None),
            P("req", "tok", None, None, None),
            P("req", "tok", None),
        ),
        out_specs=(P("req", "tok", None), P("req", None, None, None, None, "tok", None)),
        check_vma=False,
    )
```
